256 devices in a mesh: mod: 2 (over core), ctx: 32 (over z, y), dp: 4 (over x).
Axes of the slice: x: 4, y: 4, z: 8, core: 2. Of those that a mesh axis runs over, the one named last changes fastest.
Arguments:
- hidden_in: bfloat16 [4, 512, 4096], P('dp', ('mod', 'ctx')), may hold values from -6 to 6
- query_modality: int32 [4, 512], P('dp', ('mod', 'ctx')), may hold values from 0 to 1, as said below
- key_cache: bfloat16 [4, 8192, 4096], P('dp', None, 'ctx'), may hold values from -6 to 6
- value_cache: bfloat16 [4, 8192, 4096], P('dp', None, 'ctx'), may hold values from -6 to 6
- key_modality: int32 [4, 8192], P('dp'), may hold values from 0 to 1
- norm_attn: float32 [2, 4096], P('mod'), may hold values from 0.5 to 1.5
- query_weight: bfloat16 [2, 4096, 4096], P('mod', 'dp', 'ctx'), may hold values from -0.09375 to 0.09375
- query_gain: float32 [2, 4096], P('mod', 'ctx'), may hold values from 0.5 to 2.5
- key_gain: float32 [2, 4096], P(None, 'ctx'), may hold values from 0.5 to 2.5
- out_weight: bfloat16 [2, 4096, 4096], P('mod', 'ctx', 'dp'), may hold values from -0.09375 to 0.09375
- norm_ffn: float32 [2, 4096], P('mod'), may hold values from 0.5 to 1.5
- gate_weight: bfloat16 [2, 4096, 11008], P('mod', 'dp', 'ctx'), may hold values from -0.09375 to 0.09375
- up_weight: bfloat16 [2, 4096, 11008], P('mod', 'dp', 'ctx'), may hold values from -0.09375 to 0.09375
- down_weight: bfloat16 [2, 11008, 4096], P('mod', 'ctx', 'dp'), may hold values from -0.0546875 to 0.0546875
Outputs:
- mixed_out: bfloat16 [4, 512, 4096], P('dp', ('mod', 'ctx'))
The draws below stay inside these ranges and needn't reach their ends.
Inputs may be any that keep to these rules, and one draw needn't show every extreme that they name: `query_modality`: each sequence has one main modality, drawn. The slab splits into aligned blocks of 8 tokens, one block a device; in each aligned pair of blocks (2j and 2j + 1) one block holds 6 tokens of the main modality and the other 4, the rest being the other modality, so a sequence's slab holds exactly 320 tokens of its main modality.
All inputs are finite; a program needn't handle non-finite values.
Results may differ from the reference program's by a relative error of at most 0.007.
Values may be sent and summed in bfloat16 or wider, within the bound.
No kernel may reach another device: no remote copies, remote signals or barrier semaphores. Data moves between devices by JAX's collectives and lax.ppermute only.
A program may use at most 128 MiB of HBM per device.

```python
import math
import jax
import jax.numpy as jnp
from jax import lax

D = 4096
HEADS = 32
FF = 11008
HD = 128
ROWS_DEV = 8
CACHE = 8192
SEQS = 4
SLAB = 512
LCAP = 6
LOW = 4
MAIN = 320


def draw_query_modality(key, part):
    blocks = SLAB // ROWS_DEV
    key_main, key_flip, key_perm = jax.random.split(key, 3)
    main_mod = jax.random.randint(key_main, (SEQS, 1, 1), 0, 2)
    pair_flips = jax.random.randint(key_flip, (SEQS, blocks // 2, 1), 0, 2)
    first_count = jnp.where(pair_flips == 1, LCAP, LOW)
    counts = jnp.concatenate([first_count, LCAP + LOW - first_count], axis=2).reshape(SEQS, blocks, 1)
    perm_keys = jax.random.split(key_perm, SEQS * blocks)
    row_perms = jax.vmap(lambda one_key: jax.random.permutation(one_key, ROWS_DEV))(perm_keys).reshape(SEQS, blocks, ROWS_DEV)
    is_main = row_perms < counts
    modality_ids = jnp.where(is_main, main_mod, 1 - main_mod)
    return modality_ids.reshape(SEQS, SLAB).astype(jnp.int32)


def set_ends(entries, rng, smallest, top_value):
    longest = entries.shape.index(max(entries.shape))
    spots = []
    for shift in (0, 1):
        where = [jax.random.randint(jax.random.fold_in(rng, axis), (), 0, length) for axis, length in enumerate(entries.shape)]
        where[longest] = (where[longest] + shift) % entries.shape[longest]
        spots.append(tuple(where))
    return entries.at[spots[0]].set(smallest).at[spots[1]].set(top_value)


def block_scale(key, dims, shards, low, largest):
    def one(dim, parts):
        draws = jax.random.uniform(jax.random.fold_in(jax.random.fold_in(key, 6), dim), (parts,), jnp.float32, low / len(shards), largest / len(shards))
        return jnp.repeat(jnp.exp(draws), dims[dim] // parts).reshape((-1,) + (1,) * (len(dims) - dim - 1))

    gain = one(*shards[0])
    for cut in shards[1:]:
        gain = gain * one(*cut)
    return gain


def gaussian(own_key, shape, width, reach, cuts=(), kind=jnp.bfloat16):
    values = jax.random.normal(own_key, shape, jnp.float32) * width
    if len(cuts) > 0:
        values = block_scale(own_key, shape, cuts, -0.22, 0.18) * values
    return jnp.clip(values, min=-reach, max=reach).astype(kind)


def setup_inputs(seed: int = 0) -> dict:
    key_of = jax.random.split(jax.random.key(seed), 15)
    return {
        "hidden_in": gaussian(key_of[0], (SEQS, SLAB, D), 1.0, 6.0, ((0, 4), (1, 64))),
        "query_modality": draw_query_modality(jax.random.fold_in(key_of[14], 71), 0),
        "key_cache": gaussian(key_of[2], (SEQS, CACHE, D), 1.0, 6.0, ((0, 4), (2, 32))),
        "value_cache": gaussian(key_of[3], (SEQS, CACHE, D), 1.0, 6.0, ((0, 4), (2, 32))),
        "key_modality": set_ends(jax.random.randint(key_of[4], (SEQS, CACHE), 0, 2), jax.random.fold_in(key_of[4], 1), 0, 1).astype(jnp.int32),
        "norm_attn": jnp.clip(0.5 + 1.0 * jax.random.uniform(key_of[5], (2, D), jnp.float32) ** block_scale(key_of[5], (2, D), ((0, 2),), -0.2, 0.2), 0.5, 1.5),
        "query_weight": gaussian(key_of[6], (2, D, D), D ** -0.5, 0.09375, ((0, 2), (1, 4), (2, 32))),
        "query_gain": jnp.clip(jnp.exp(math.log(2.5) - 1.609438 * jax.random.uniform(key_of[7], (2, D), jnp.float32) ** block_scale(key_of[7], (2, D), ((0, 2), (1, 32)), -0.2, 0.2)), 0.5, 2.5),
        "key_gain": jnp.clip(jnp.exp(math.log(2.5) - 1.609438 * jax.random.uniform(key_of[8], (2, D), jnp.float32) ** block_scale(key_of[8], (2, D), ((1, 32),), -0.2, 0.2)), 0.5, 2.5),
        "out_weight": gaussian(key_of[9], (2, D, D), D ** -0.5, 0.09375, ((0, 2), (1, 32), (2, 4))),
        "norm_ffn": jnp.clip(0.5 + 1.0 * jax.random.uniform(key_of[10], (2, D), jnp.float32) ** block_scale(key_of[10], (2, D), ((0, 2),), -0.2, 0.2), 0.5, 1.5),
        "gate_weight": gaussian(key_of[11], (2, D, FF), D ** -0.5, 0.09375, ((0, 2), (1, 4), (2, 32))),
        "up_weight": gaussian(key_of[12], (2, D, FF), D ** -0.5, 0.09375, ((0, 2), (1, 4), (2, 32))),
        "down_weight": gaussian(key_of[13], (2, FF, D), FF ** -0.5, 0.0546875, ((0, 2), (1, 32), (2, 4))),
    }


epsilon = 1e-05

def rms_scale(values, scales):
    inverse = lax.rsqrt(lax.optimization_barrier(jnp.mean(values * values, axis=-1, keepdims=True)) + epsilon)
    return values * inverse * scales

def attend_head(query_head, key_head, value_head, query_pos):
    scores = jnp.dot(query_head, key_head.T, preferred_element_type=jnp.float32) * (1.0 / math.sqrt(HD))
    allowed = jnp.arange(CACHE, dtype=jnp.int32)[None, :] <= query_pos[:, None]
    scores = jnp.where(allowed, scores, -1e+30)
    row_max = lax.optimization_barrier(jnp.max(scores, axis=-1, keepdims=True))
    weights = jnp.exp(scores - row_max)
    row_total = lax.optimization_barrier(jnp.sum(weights, axis=-1, keepdims=True))
    summed = jnp.dot(weights.astype(jnp.bfloat16), value_head, preferred_element_type=jnp.float32)
    return (summed / row_total).astype(jnp.bfloat16)

def reference(hidden_in, query_modality, key_cache, value_cache, key_modality, norm_attn, query_weight, query_gain, key_gain, out_weight, norm_ffn, gate_weight, up_weight, down_weight):
    query_pos = CACHE - SLAB + jnp.arange(SLAB, dtype=jnp.int32)
    outputs = []
    for seq_index in range(SEQS):
        modality_ids = query_modality[seq_index]
        sorted_rows = jnp.argsort(modality_ids, stable=True).astype(jnp.int32)
        group_index = (sorted_rows[:MAIN], sorted_rows[SLAB - MAIN:])
        rows_all = hidden_in[seq_index].astype(jnp.float32)
        queries = jnp.zeros((SLAB, HEADS, HD), jnp.float32)
        for modality in range(2):
            row_index = group_index[modality]
            keep_rows = (modality_ids[row_index] == modality)[:, None, None]
            normed = rms_scale(rows_all[row_index], norm_attn[modality]).astype(jnp.bfloat16)
            projected = jnp.dot(normed, query_weight[modality], preferred_element_type=jnp.float32).reshape(MAIN, HEADS, HD)
            normal_q = rms_scale(projected, query_gain[modality].reshape(HEADS, HD))
            queries = queries.at[row_index].set(jnp.where(keep_rows, normal_q, queries[row_index]))
        queries = queries.astype(jnp.bfloat16)
        key_scale = jnp.where(key_modality[seq_index][:, None] == 0, key_gain[0][None, :], key_gain[1][None, :]).reshape(CACHE, HEADS, HD)
        key_rows = rms_scale(key_cache[seq_index].astype(jnp.float32).reshape(CACHE, HEADS, HD), key_scale).astype(jnp.bfloat16)
        value_rows = value_cache[seq_index].reshape(CACHE, HEADS, HD)
        head_out = lax.map(lambda triple: attend_head(triple[0], triple[1], triple[2], query_pos), (queries.transpose(1, 0, 2), key_rows.transpose(1, 0, 2), value_rows.transpose(1, 0, 2)))
        head_out = head_out.transpose(1, 0, 2).reshape(SLAB, D)
        mixed_rows = jnp.zeros((SLAB, D), jnp.bfloat16)
        for modality in range(2):
            row_index = group_index[modality]
            keep_rows = (modality_ids[row_index] == modality)[:, None]
            attention = jnp.dot(head_out[row_index], out_weight[modality], preferred_element_type=jnp.float32)
            residual = rows_all[row_index] + attention
            normed = rms_scale(residual, norm_ffn[modality]).astype(jnp.bfloat16)
            gate_val = jnp.dot(normed, gate_weight[modality], preferred_element_type=jnp.float32)
            up_val = jnp.dot(normed, up_weight[modality], preferred_element_type=jnp.float32)
            activated = (jax.nn.silu(gate_val) * up_val).astype(jnp.bfloat16)
            result = (residual + jnp.dot(activated, down_weight[modality], preferred_element_type=jnp.float32)).astype(jnp.bfloat16)
            mixed_rows = mixed_rows.at[row_index].set(jnp.where(keep_rows, result, mixed_rows[row_index]))
        outputs.append(mixed_rows)
    return jnp.stack(outputs)
```

```python
import functools
import math

import jax
import jax.numpy as jnp
from jax import lax
from jax.experimental import pallas as pl
from jax.experimental.pallas import tpu as pltpu
from jax.sharding import PartitionSpec as P

HD = 128
Y = 4
KEY_TILE = 1024

epsilon = 1e-05


def rms_scale(values, scales):
    inverse = lax.rsqrt(jnp.mean(values * values, axis=-1, keepdims=True) + epsilon)
    return values * inverse * scales


def swap_core(value):
    return lax.ppermute(value, "mod", [(0, 1), (1, 0)])


def from_y(value, shift, n_ctx):
    pairs = [(z * Y + (y + shift) % Y, z * Y + y) for z in range(n_ctx // Y) for y in range(Y)]
    return lax.ppermute(value, "ctx", pairs)


def from_z(value, shift, n_ctx):
    n_z = n_ctx // Y
    pairs = [(((z + shift) % n_z) * Y + y, z * Y + y) for z in range(n_z) for y in range(Y)]
    return lax.ppermute(value, "ctx", pairs)


def gather_tokens(block, n_ctx):
    n_z = n_ctx // Y
    top = n_z // 2
    here = jnp.concatenate([block] + [from_y(block, dy, n_ctx) for dy in range(1, Y)], axis=0)
    half = here.shape[0] // 2
    blocks = {0: here}
    ahead = behind = here
    for step in range(1, top):
        ahead = from_z(ahead, 1, n_ctx)
        behind = from_z(behind, -1, n_ctx)
        blocks[step] = ahead
        blocks[n_z - step] = behind
    blocks[top] = jnp.concatenate(
        [from_z(ahead[:half], 1, n_ctx), from_z(behind[half:], -1, n_ctx)], axis=0
    )
    return jnp.concatenate([blocks[dz] for dz in range(n_z)], axis=0)


def scatter_sums(terms, n_ctx):
    n_z = n_ctx // Y
    top = n_z // 2
    terms = terms.reshape(n_z, -1, terms.shape[-1])
    rows = terms.shape[1]
    half = rows // 2

    def narrow(value):
        return value.astype(jnp.bfloat16)

    ahead = from_z(narrow(terms[top][:half]), -1, n_ctx).astype(jnp.float32)
    behind = from_z(narrow(terms[top][half:]), 1, n_ctx).astype(jnp.float32)
    for step in range(top - 1, 0, -1):
        own_ahead, own_behind = terms[step], terms[n_z - step]
        if step == top - 1:
            ahead = jnp.concatenate([ahead + own_ahead[:half], own_ahead[half:]], axis=0)
            behind = jnp.concatenate([own_behind[:half], behind + own_behind[half:]], axis=0)
        else:
            ahead = ahead + own_ahead
            behind = behind + own_behind
        ahead = from_z(narrow(ahead), -1, n_ctx).astype(jnp.float32)
        behind = from_z(narrow(behind), 1, n_ctx).astype(jnp.float32)
    total = (terms[0] + ahead + behind).reshape(Y, rows // Y, -1)
    result = total[0]
    for dy in range(1, Y):
        result = result + from_y(narrow(total[dy]), -dy, n_ctx).astype(jnp.float32)
    return result


def attend_kernel(slab_start, query_ref, key_ref, value_ref, position_ref, out_ref, total):
    step = pl.program_id(0)
    last = pl.num_programs(0) - 1
    sub = KEY_TILE // 2

    @pl.when(step == 0)
    def _():
        total[...] = jnp.zeros_like(total)

    def part(index, masked):
        keys = key_ref[index * sub : (index + 1) * sub, :]
        scores = lax.dot_general(
            query_ref[...], keys, (((1,), (1,)), ((), ())), preferred_element_type=jnp.float32
        )
        weights = jnp.exp2(scores)
        if masked:
            at = step * KEY_TILE + index * sub
            ids = at + lax.broadcasted_iota(jnp.int32, scores.shape, 1)
            weights = jnp.where(ids <= position_ref[...], weights, 0.0)
        return jnp.dot(
            weights.astype(jnp.bfloat16),
            value_ref[index * sub : (index + 1) * sub, :],
            preferred_element_type=jnp.float32,
        )

    first_masked = slab_start // KEY_TILE

    @pl.when(step < first_masked)
    def _():
        total[...] += part(0, False) + part(1, False)

    @pl.when(step >= first_masked)
    def _():
        total[...] += part(0, True) + part(1, True)

    @pl.when(step == last)
    def _():
        summed = total[...]
        out_ref[...] = (summed[:, :HD] / summed[:, HD:]).astype(jnp.bfloat16)


def attend(queries, keys, values, positions, slab_start):
    rows = queries.shape[0]
    cache = keys.shape[0]
    return pl.pallas_call(
        functools.partial(attend_kernel, slab_start),
        grid=(cache // KEY_TILE,),
        in_specs=[
            pl.BlockSpec((rows, HD), lambda i: (0, 0)),
            pl.BlockSpec((KEY_TILE, HD), lambda i: (i, 0)),
            pl.BlockSpec((KEY_TILE, 2 * HD), lambda i: (i, 0)),
            pl.BlockSpec((rows, 1), lambda i: (0, 0)),
        ],
        out_specs=pl.BlockSpec((rows, HD), lambda i: (0, 0)),
        out_shape=jax.ShapeDtypeStruct((rows, HD), jnp.bfloat16),
        scratch_shapes=[pltpu.VMEM((rows, 2 * HD), jnp.float32)],
        compiler_params=pltpu.CompilerParams(vmem_limit_bytes=24 * 1024 * 1024),
        cost_estimate=pl.CostEstimate(
            flops=6 * rows * cache * HD,
            bytes_accessed=6 * cache * HD,
            transcendentals=rows * cache,
        ),
        name="attend",
    )(queries, keys, values, positions)


def per_device(
    hidden_in,
    query_modality,
    key_cache,
    value_cache,
    key_modality,
    norm_attn,
    query_weight,
    query_gain,
    key_gain,
    out_weight,
    norm_ffn,
    gate_weight,
    up_weight,
    down_weight,
):
    core = lax.axis_index("mod")
    ctx_index = lax.axis_index("ctx")
    n_ctx = lax.axis_size("ctx")
    n_z = n_ctx // Y
    rows_dev, width = hidden_in.shape[1:]
    cache_len = key_cache.shape[1]
    slab_len = rows_dev * n_ctx * lax.axis_size("mod")
    slab_start = cache_len - slab_len

    def both(gathered):
        return gathered, swap_core(gathered)

    q_own, q_other = both(lax.all_gather(query_weight[0], "dp", axis=0, tiled=True))
    o_own, o_other = both(lax.all_gather(out_weight[0], "dp", axis=1, tiled=True))
    g_own, g_other = both(lax.all_gather(gate_weight[0], "dp", axis=0, tiled=True))
    u_own, u_other = both(lax.all_gather(up_weight[0], "dp", axis=0, tiled=True))
    d_own, d_other = both(lax.all_gather(down_weight[0], "dp", axis=1, tiled=True))

    gains_own = jnp.concatenate([norm_attn, norm_ffn, query_gain], axis=1)
    gains_other = swap_core(gains_own)

    home_own = (query_modality[0] == core)[:, None]
    hidden = hidden_in[0].astype(jnp.float32)
    gain = jnp.where(home_own, gains_own[:, :width], gains_other[:, :width])
    normed = rms_scale(hidden, gain).astype(jnp.bfloat16)
    flags = jnp.broadcast_to(query_modality[0][:, None].astype(jnp.bfloat16), (rows_dev, HD))
    slab = gather_tokens(jnp.concatenate([normed, flags], axis=1), n_ctx)
    slab_own = slab[:, width : width + 1] == core.astype(jnp.bfloat16)
    slab = slab[:, :width]

    z_here, y_here = ctx_index // Y, ctx_index % Y
    at_z = (z_here + jnp.arange(n_z, dtype=jnp.int32)) % n_z
    at_y = (y_here + jnp.arange(Y, dtype=jnp.int32)) % Y
    block = core * n_ctx + at_z[:, None] * Y + at_y[None, :]
    positions = block[:, :, None] * rows_dev + jnp.arange(rows_dev, dtype=jnp.int32)
    positions = slab_start + positions.reshape(-1, 1)

    key_scale = jnp.where(
        key_modality[0][:, None] == 0, key_gain[0][None, :], key_gain[1][None, :]
    )
    keys = rms_scale(key_cache[0].astype(jnp.float32), key_scale).astype(jnp.bfloat16)
    values = jnp.concatenate(
        [value_cache[0], jnp.ones((cache_len, HD), jnp.bfloat16)], axis=1
    )

    projected = jnp.where(
        slab_own,
        jnp.dot(slab, q_own, preferred_element_type=jnp.float32),
        jnp.dot(slab, q_other, preferred_element_type=jnp.float32),
    )
    q_gain = jnp.where(slab_own, gains_own[:, 2 * width :], gains_other[:, 2 * width :])
    queries = rms_scale(projected, q_gain) * (math.log2(math.e) / math.sqrt(HD))
    heads = attend(queries.astype(jnp.bfloat16), keys, values, positions, slab_start)

    zero = jnp.zeros((), jnp.bfloat16)
    attended = scatter_sums(
        jnp.dot(jnp.where(slab_own, heads, zero), o_own, preferred_element_type=jnp.float32)
        + jnp.dot(jnp.where(slab_own, zero, heads), o_other, preferred_element_type=jnp.float32),
        n_ctx,
    )
    residual = hidden + attended
    gain = jnp.where(
        home_own, gains_own[:, width : 2 * width], gains_other[:, width : 2 * width]
    )
    slab = gather_tokens(rms_scale(residual, gain).astype(jnp.bfloat16), n_ctx)

    def expand(own, other):
        return jnp.where(
            slab_own,
            jnp.dot(slab, own, preferred_element_type=jnp.float32),
            jnp.dot(slab, other, preferred_element_type=jnp.float32),
        )

    activated = (jax.nn.silu(expand(g_own, g_other)) * expand(u_own, u_other)).astype(jnp.bfloat16)
    ffn = scatter_sums(
        jnp.dot(jnp.where(slab_own, activated, zero), d_own, preferred_element_type=jnp.float32)
        + jnp.dot(jnp.where(slab_own, zero, activated), d_other, preferred_element_type=jnp.float32),
        n_ctx,
    )
    return (residual + ffn).astype(jnp.bfloat16)[None]


def solution(mesh):
    placed = (
        P("dp", ("mod", "ctx"), None),
        P("dp", ("mod", "ctx")),
        P("dp", None, "ctx"),
        P("dp", None, "ctx"),
        P("dp", None),
        P("mod", None),
        P("mod", "dp", "ctx"),
        P("mod", "ctx"),
        P(None, "ctx"),
        P("mod", "ctx", "dp"),
        P("mod", None),
        P("mod", "dp", "ctx"),
        P("mod", "dp", "ctx"),
        P("mod", "ctx", "dp"),
    )
    return jax.shard_map(
        per_device,
        mesh=mesh,
        in_specs=placed,
        out_specs=P("dp", ("mod", "ctx"), None),
        check_vma=False,
    )
```

```python
import functools
import math

import jax
import jax.numpy as jnp
from jax import lax
from jax.experimental import pallas as pl
from jax.experimental.pallas import tpu as pltpu
from jax.sharding import PartitionSpec as P

HD = 128
Y = 4
KEY_TILE = 1024
TILE = 16

epsilon = 1e-05


def rms_scale(values, scales):
    inverse = lax.rsqrt(jnp.mean(values * values, axis=-1, keepdims=True) + epsilon)
    return values * inverse * scales


def swap_core(value):
    return lax.ppermute(value, "mod", [(0, 1), (1, 0)])


def from_x(value, shift):
    n_x = lax.axis_size("dp")
    return lax.ppermute(value, "dp", [((i + shift) % n_x, i) for i in range(n_x)])


def after(value, anchor):
    return lax.optimization_barrier((value, anchor))[0]


def from_y(value, shift, n_ctx):
    pairs = [(z * Y + (y + shift) % Y, z * Y + y) for z in range(n_ctx // Y) for y in range(Y)]
    return lax.ppermute(value, "ctx", pairs)


def from_z(value, shift, n_ctx):
    n_z = n_ctx // Y
    pairs = [(((z + shift) % n_z) * Y + y, z * Y + y) for z in range(n_z) for y in range(Y)]
    return lax.ppermute(value, "ctx", pairs)


def gather_tokens(block, n_ctx):
    n_z = n_ctx // Y
    top = n_z // 2
    here = jnp.concatenate([block] + [from_y(block, dy, n_ctx) for dy in range(1, Y)], axis=0)
    half = here.shape[0] // 2
    blocks = {0: here}
    ahead = behind = here
    for step in range(1, top):
        ahead = from_z(ahead, 1, n_ctx)
        behind = from_z(behind, -1, n_ctx)
        blocks[step] = ahead
        blocks[n_z - step] = behind
    blocks[top] = jnp.concatenate(
        [from_z(ahead[:half], 1, n_ctx), from_z(behind[half:], -1, n_ctx)], axis=0
    )
    return jnp.concatenate([blocks[dz] for dz in range(n_z)], axis=0)


def scatter_sums(terms, n_ctx):
    n_z = n_ctx // Y
    top = n_z // 2
    terms = terms.reshape(n_z, -1, terms.shape[-1])
    rows = terms.shape[1]
    half = rows // 2

    def narrow(value):
        return value.astype(jnp.bfloat16)

    ahead = from_z(narrow(terms[top][:half]), -1, n_ctx).astype(jnp.float32)
    behind = from_z(narrow(terms[top][half:]), 1, n_ctx).astype(jnp.float32)
    for step in range(top - 1, 0, -1):
        own_ahead, own_behind = terms[step], terms[n_z - step]
        if step == top - 1:
            ahead = jnp.concatenate([ahead + own_ahead[:half], own_ahead[half:]], axis=0)
            behind = jnp.concatenate([own_behind[:half], behind + own_behind[half:]], axis=0)
        else:
            ahead = ahead + own_ahead
            behind = behind + own_behind
        ahead = from_z(narrow(ahead), -1, n_ctx).astype(jnp.float32)
        behind = from_z(narrow(behind), 1, n_ctx).astype(jnp.float32)
    total = (terms[0] + ahead + behind).reshape(Y, rows // Y, -1)
    result = total[0]
    for dy in range(1, Y):
        result = result + from_y(narrow(total[dy]), -dy, n_ctx).astype(jnp.float32)
    return result


def matmul(left, right):
    return jnp.dot(left, right, preferred_element_type=jnp.float32)


def matmul_t(left, right):
    return lax.dot_general(
        left, right, (((1,), (1,)), ((), ())), preferred_element_type=jnp.float32
    )


def attend_kernel(
    slab_start,
    parts,
    slab_ref,
    own_ref,
    position_ref,
    gain_ref,
    qo_own_ref,
    qo_other_ref,
    key_ref,
    value_ref,
    out_ref,
    query,
    summed,
    row_total,
):
    step = pl.program_id(0)
    last = pl.num_programs(0) - 1
    part = qo_own_ref.shape[2]
    sub = KEY_TILE // 2
    own = own_ref[...] > 0.5

    @pl.when(step == 0)
    def _():
        projected_own = projected_other = 0.0
        for k in range(parts):
            rows = slab_ref[:, k * part : (k + 1) * part]
            projected_own = projected_own + matmul_t(rows, qo_own_ref[k, :HD, :])
            projected_other = projected_other + matmul_t(rows, qo_other_ref[k, :HD, :])
        projected = jnp.where(own, projected_own, projected_other)
        gain = jnp.where(own, gain_ref[0:1, :], gain_ref[1:2, :])
        normed = rms_scale(projected, gain)
        query[...] = (normed * (math.log2(math.e) / math.sqrt(HD))).astype(jnp.bfloat16)
        summed[...] = jnp.zeros_like(summed)
        row_total[...] = jnp.zeros_like(row_total)

    def add_keys(masked):
        for index in range(KEY_TILE // sub):
            scores = matmul_t(query[...], key_ref[index * sub : (index + 1) * sub, :])
            weights = jnp.exp2(scores)
            if masked:
                at = step * KEY_TILE + index * sub
                ids = at + lax.broadcasted_iota(jnp.int32, scores.shape, 1)
                weights = jnp.where(ids <= position_ref[...], weights, 0.0)
            folded = weights[:, :HD]
            for lane in range(HD, sub, HD):
                folded = folded + weights[:, lane : lane + HD]
            row_total[...] += folded
            summed[...] += matmul(
                weights.astype(jnp.bfloat16), value_ref[index * sub : (index + 1) * sub, :]
            )

    first_masked = slab_start // KEY_TILE

    @pl.when(step < first_masked)
    def _():
        add_keys(False)

    @pl.when(step >= first_masked)
    def _():
        add_keys(True)

    @pl.when(step == last)
    def _():
        totals = jnp.sum(row_total[...], axis=-1, keepdims=True)
        heads = (summed[...] / totals).astype(jnp.bfloat16)
        zero = jnp.zeros_like(heads)
        heads_own = jnp.where(own, heads, zero)
        heads_other = jnp.where(own, zero, heads)
        for k in range(parts):
            out_ref[:, k * part : (k + 1) * part] = matmul(
                heads_own, qo_own_ref[k, HD:, :]
            ) + matmul(heads_other, qo_other_ref[k, HD:, :])


def attend(slab, own, positions, gains, qo_own, qo_other, keys, values, slab_start):
    rows, width = slab.shape
    cache = keys.shape[0]
    parts = qo_own.shape[0]

    def whole(array):
        return pl.BlockSpec(array.shape, lambda i: (0,) * array.ndim)

    return pl.pallas_call(
        functools.partial(attend_kernel, slab_start, parts),
        grid=(cache // KEY_TILE,),
        in_specs=[
            whole(slab),
            whole(own),
            whole(positions),
            whole(gains),
            whole(qo_own),
            whole(qo_other),
            pl.BlockSpec((KEY_TILE, HD), lambda i: (i, 0)),
            pl.BlockSpec((KEY_TILE, HD), lambda i: (i, 0)),
        ],
        out_specs=pl.BlockSpec((rows, parts * qo_own.shape[2]), lambda i: (0, 0)),
        out_shape=jax.ShapeDtypeStruct((rows, parts * qo_own.shape[2]), jnp.float32),
        scratch_shapes=[
            pltpu.VMEM((rows, HD), jnp.bfloat16),
            pltpu.VMEM((rows, HD), jnp.float32),
            pltpu.VMEM((rows, HD), jnp.float32),
        ],
        compiler_params=pltpu.CompilerParams(vmem_limit_bytes=40 * 1024 * 1024),
        cost_estimate=pl.CostEstimate(
            flops=4 * rows * cache * HD + 8 * rows * width * HD,
            bytes_accessed=4 * cache * HD + 8 * width * HD + 6 * rows * width,
            transcendentals=rows * cache,
        ),
        name="attend",
    )(slab, own, positions, gains, qo_own, qo_other, keys, values)


def ffn_kernel(units, slab_ref, own_ref, *rest):
    pieces, (out_ref, weights, gate_up, sems) = rest[:10], rest[10:]
    part = weights.shape[3]
    cut = part // 2
    own = own_ref[...] > 0.5
    places = ((0, 0, part), (1, 0, part), (2, 0, cut), (2, cut, part), (3, 0, part))
    order = (0, 1, 4, 2, 3)
    copies = {}
    for which in order:
        slot, low, high = places[which]
        for group in range(2):
            copy = pltpu.make_async_copy(
                pieces[5 * group + which],
                weights.at[group, slot, :, low:high],
                sems.at[5 * group + which],
            )
            copy.start()
            copies[which, group] = copy
    first = True
    for which in order:
        slot, low, high = places[which]
        rows = slab_ref[:, slot * part + low : slot * part + high]
        for group in range(2):
            copies[which, group].wait()
            for kind in range(2):
                product = matmul_t(
                    rows, weights[group, slot, kind * units : (kind + 1) * units, low:high]
                )
                if first:
                    gate_up[group, kind] = product
                else:
                    gate_up[group, kind] += product
        first = False
    gate = jnp.where(own, gate_up[0, 0], gate_up[1, 0])
    up = jnp.where(own, gate_up[0, 1], gate_up[1, 1])
    activated = (gate / (1.0 + jnp.exp(-gate)) * up).astype(jnp.bfloat16)
    zero = jnp.zeros_like(activated)
    activated_own = jnp.where(own, activated, zero)
    activated_other = jnp.where(own, zero, activated)
    for slot in range(4):
        out_ref[:, slot * part : (slot + 1) * part] = matmul(
            activated_own, weights[0, slot, 2 * units :, :]
        ) + matmul(activated_other, weights[1, slot, 2 * units :, :])


def feed_forward(slab, own, pieces_own, pieces_other):
    rows, width = slab.shape
    stacked, part = pieces_own[0].shape
    units = stacked // 3
    return pl.pallas_call(
        functools.partial(ffn_kernel, units),
        in_specs=[pl.BlockSpec(memory_space=pltpu.VMEM)] * 2
        + [pl.BlockSpec(memory_space=pl.ANY)] * 10,
        out_specs=pl.BlockSpec(memory_space=pltpu.VMEM),
        out_shape=jax.ShapeDtypeStruct((rows, width), jnp.float32),
        scratch_shapes=[
            pltpu.VMEM((2, 4, stacked, part), jnp.bfloat16),
            pltpu.VMEM((2, 2, rows, units), jnp.float32),
            pltpu.SemaphoreType.DMA((10,)),
        ],
        compiler_params=pltpu.CompilerParams(vmem_limit_bytes=40 * 1024 * 1024),
        cost_estimate=pl.CostEstimate(
            flops=4 * rows * stacked * width,
            bytes_accessed=4 * stacked * width + 6 * rows * width,
            transcendentals=rows * units,
        ),
        name="feed_forward",
    )(slab, own, *pieces_own, *pieces_other)


def per_device(
    hidden_in,
    query_modality,
    key_cache,
    value_cache,
    key_modality,
    norm_attn,
    query_weight,
    query_gain,
    key_gain,
    out_weight,
    norm_ffn,
    gate_weight,
    up_weight,
    down_weight,
):
    core = lax.axis_index("mod")
    ctx_index = lax.axis_index("ctx")
    n_ctx = lax.axis_size("ctx")
    n_x = lax.axis_size("dp")
    n_z = n_ctx // Y
    rows_dev, width = hidden_in.shape[1:]
    part = width // n_x
    units = down_weight.shape[1]
    cache_len = key_cache.shape[1]
    slab_len = rows_dev * n_ctx * lax.axis_size("mod")
    slab_start = cache_len - slab_len
    turn = lax.axis_index("dp") * part

    gains_own = jnp.concatenate([norm_attn, norm_ffn], axis=0)
    q_gain_own = query_gain
    packed = jnp.concatenate([gains_own.reshape(1, -1), q_gain_own], axis=1)
    packed_other = swap_core(packed)
    gains = jnp.concatenate([gains_own, packed_other[:, : 2 * width].reshape(2, width)], axis=0)
    gains = jnp.roll(gains, -turn, axis=1)
    q_gains = jnp.concatenate([q_gain_own, packed_other[:, 2 * width :]], axis=0)

    home_own = (query_modality[0] == core)[:, None]
    hidden = jnp.roll(hidden_in[0], -turn, axis=1).astype(jnp.float32)
    normed = rms_scale(hidden, jnp.where(home_own, gains[0:1], gains[2:3])).astype(jnp.bfloat16)
    flags = jnp.broadcast_to(query_modality[0][:, None].astype(jnp.bfloat16), (rows_dev, HD))
    block = jnp.concatenate([normed, flags], axis=1)

    qo_here = jnp.concatenate([query_weight[0].T, out_weight[0]], axis=0)
    qo_here = after(qo_here, block)
    qo_own = jnp.stack([qo_here] + [from_x(qo_here, k) for k in range(1, n_x)])
    qo_other = swap_core(qo_own)

    slab = gather_tokens(block, n_ctx)
    slab_own = (slab[:, width : width + 1] == core.astype(jnp.bfloat16)).astype(jnp.float32)
    slab = slab[:, :width]

    key_rows = after(key_cache[0], block)
    key_scale = jnp.where(
        key_modality[0][:, None] == 0, key_gain[0][None, :], key_gain[1][None, :]
    )
    keys = rms_scale(key_rows.astype(jnp.float32), key_scale).astype(jnp.bfloat16)

    padding = ((0, -units % TILE), (0, 0))
    ffn_here = jnp.concatenate(
        [
            jnp.pad(weight, padding)
            for weight in (gate_weight[0].T, up_weight[0].T, down_weight[0])
        ],
        axis=0,
    )
    ffn_here = after(ffn_here, slab)
    ffn_next, ffn_last = from_x(ffn_here, 1), from_x(ffn_here, 3)

    z_here, y_here = ctx_index // Y, ctx_index % Y
    at_z = (z_here + jnp.arange(n_z, dtype=jnp.int32)) % n_z
    at_y = (y_here + jnp.arange(Y, dtype=jnp.int32)) % Y
    at = core * n_ctx + at_z[:, None] * Y + at_y[None, :]
    positions = at[:, :, None] * rows_dev + jnp.arange(rows_dev, dtype=jnp.int32)
    positions = slab_start + positions.reshape(-1, 1)
    attended = attend(
        slab, slab_own, positions, q_gains, qo_own, qo_other, keys, value_cache[0], slab_start
    )
    attended = scatter_sums(attended, n_ctx)

    residual = hidden + attended
    normed = rms_scale(residual, jnp.where(home_own, gains[1:2], gains[3:4])).astype(jnp.bfloat16)

    cut = part // 2
    pieces_own = [
        ffn_here,
        ffn_next,
        from_x(after(ffn_next[:, :cut], attended), 1),
        from_x(after(ffn_last[:, cut:], attended), 3),
        ffn_last,
    ]
    pieces_other = [swap_core(piece) for piece in pieces_own]

    slab = gather_tokens(normed, n_ctx)
    mixed = feed_forward(slab, slab_own, pieces_own, pieces_other)
    mixed = (residual + scatter_sums(mixed, n_ctx)).astype(jnp.bfloat16)
    return jnp.roll(mixed, turn, axis=1)[None]


def solution(mesh):
    placed = (
        P("dp", ("mod", "ctx"), None),
        P("dp", ("mod", "ctx")),
        P("dp", None, "ctx"),
        P("dp", None, "ctx"),
        P("dp", None),
        P("mod", None),
        P("mod", "dp", "ctx"),
        P("mod", "ctx"),
        P(None, "ctx"),
        P("mod", "ctx", "dp"),
        P("mod", None),
        P("mod", "dp", "ctx"),
        P("mod", "dp", "ctx"),
        P("mod", "ctx", "dp"),
    )
    return jax.shard_map(
        per_device,
        mesh=mesh,
        in_specs=placed,
        out_specs=P("dp", ("mod", "ctx"), None),
        check_vma=False,
    )
```

```python
import functools
import math

import jax
import jax.numpy as jnp
from jax import lax
from jax.experimental import pallas as pl
from jax.experimental.pallas import tpu as pltpu
from jax.sharding import PartitionSpec as P

HD = 128
Y = 4
KEY_TILE = 1024
TILE = 16

epsilon = 1e-05


def rms_scale(values, scales):
    inverse = lax.rsqrt(jnp.mean(values * values, axis=-1, keepdims=True) + epsilon)
    return values * inverse * scales


def swap_core(value):
    return lax.ppermute(value, "mod", [(0, 1), (1, 0)])


def from_x(value, shift):
    n_x = lax.axis_size("dp")
    return lax.ppermute(value, "dp", [((i + shift) % n_x, i) for i in range(n_x)])


def after(value, anchor):
    return lax.optimization_barrier((value, anchor))[0]


def from_yz(value, shift_y, shift_z):
    n_z = lax.axis_size("ctx") // Y
    pairs = [
        (((z + shift_z) % n_z) * Y + (y + shift_y) % Y, z * Y + y)
        for z in range(n_z)
        for y in range(Y)
    ]
    return lax.ppermute(value, "ctx", pairs)


def from_y(value, shift):
    return from_yz(value, shift, 0)


def from_z(value, shift):
    return from_yz(value, 0, shift)


def gather_y(block):
    return jnp.concatenate([block] + [from_y(block, dy) for dy in range(1, Y)], axis=0)


def gather_z(here, hooks):
    n_z = lax.axis_size("ctx") // Y
    top = n_z // 2
    half = here.shape[0] // 2
    blocks = {0: here}
    ahead = behind = here
    for step in range(1, top):
        ahead = from_z(ahead, 1)
        behind = from_z(behind, -1)
        if step in hooks:
            ahead = hooks[step](ahead)
        blocks[step] = ahead
        blocks[n_z - step] = behind
    far = [from_z(ahead[:half], 1), from_z(behind[half:], -1)]
    near = [blocks[dz] for dz in range(n_z) if dz != top]
    return near[:top] + far + near[top:]


def narrow(value):
    return value.astype(jnp.bfloat16)


def wide(value):
    return value.astype(jnp.float32)


def scatter_z(terms, hooks):
    n_z = lax.axis_size("ctx") // Y
    top = n_z // 2
    terms = terms.reshape(n_z, -1, terms.shape[-1])
    half = terms.shape[1] // 2
    ahead = from_z(terms[top][:half], -1)
    behind = from_z(terms[top][half:], 1)
    for step in range(top - 1, 0, -1):
        own_ahead, own_behind = terms[step], terms[n_z - step]
        if step == top - 1:
            first = narrow(wide(ahead) + wide(own_ahead[:half]))
            ahead = jnp.concatenate([first, own_ahead[half:]], axis=0)
            first = narrow(wide(behind) + wide(own_behind[half:]))
            behind = jnp.concatenate([own_behind[:half], first], axis=0)
        else:
            ahead = narrow(wide(ahead) + wide(own_ahead))
            behind = narrow(wide(behind) + wide(own_behind))
        ahead = from_z(ahead, -1)
        behind = from_z(behind, 1)
        if step in hooks:
            ahead = hooks[step](ahead)
    return wide(terms[0]) + wide(ahead) + wide(behind)


def scatter_y(total):
    total = total.reshape(Y, -1, total.shape[-1])
    result = total[0]
    for dy in range(1, Y):
        result = result + wide(from_y(narrow(total[dy]), -dy))
    return result


def sum_y(total):
    sent = narrow(total)
    rows = total.shape[0] // Y
    result = total
    for dy in range(1, Y):
        result = result + jnp.roll(wide(from_y(sent, dy)), dy * rows, axis=0)
    return result


def matmul(left, right):
    return jnp.dot(left, right, preferred_element_type=jnp.float32)


def matmul_t(left, right):
    return lax.dot_general(
        left, right, (((1,), (1,)), ((), ())), preferred_element_type=jnp.float32
    )


def fill(slab, blocks):
    low = 0
    for block in blocks:
        slab[low : low + block.shape[0], :] = block[...]
        low += block.shape[0]


def attend_kernel(
    slab_start,
    parts,
    core_ref,
    position_ref,
    gain_ref,
    qo_own_ref,
    qo_other_ref,
    key_ref,
    value_ref,
    *rest,
):
    *blocks, out_ref, own_ref, slab_ref, query, summed, row_total = rest
    step = pl.program_id(0)
    last = pl.num_programs(0) - 1
    part = qo_own_ref.shape[2]
    width = parts * part
    sub = KEY_TILE // 2

    def is_own():
        return slab_ref[:, width : width + 1].astype(jnp.float32) == core_ref[...]

    @pl.when(step == 0)
    def _():
        fill(slab_ref, blocks)
        own = is_own()
        projected_own = projected_other = 0.0
        for k in range(parts):
            rows = slab_ref[:, k * part : (k + 1) * part]
            projected_own = projected_own + matmul_t(rows, qo_own_ref[k, :HD, :])
            projected_other = projected_other + matmul_t(rows, qo_other_ref[k, :HD, :])
        projected = jnp.where(own, projected_own, projected_other)
        gain = jnp.where(own, gain_ref[0:1, :], gain_ref[1:2, :])
        normed = rms_scale(projected, gain)
        query[...] = (normed * (math.log2(math.e) / math.sqrt(HD))).astype(jnp.bfloat16)
        summed[...] = jnp.zeros_like(summed)
        row_total[...] = jnp.zeros_like(row_total)

    def add_keys(masked):
        for index in range(KEY_TILE // sub):
            scores = matmul_t(query[...], key_ref[index * sub : (index + 1) * sub, :])
            weights = jnp.exp2(scores)
            if masked:
                at = step * KEY_TILE + index * sub
                ids = at + lax.broadcasted_iota(jnp.int32, scores.shape, 1)
                weights = jnp.where(ids <= position_ref[...], weights, 0.0)
            folded = weights[:, :HD]
            for lane in range(HD, sub, HD):
                folded = folded + weights[:, lane : lane + HD]
            row_total[...] += folded
            summed[...] += matmul(
                weights.astype(jnp.bfloat16), value_ref[index * sub : (index + 1) * sub, :]
            )

    first_masked = slab_start // KEY_TILE

    @pl.when(step < first_masked)
    def _():
        add_keys(False)

    @pl.when(step >= first_masked)
    def _():
        add_keys(True)

    @pl.when(step == last)
    def _():
        totals = jnp.sum(row_total[...], axis=-1, keepdims=True)
        heads = (summed[...] / totals).astype(jnp.bfloat16)
        zero = jnp.zeros_like(heads)
        own = is_own()
        own_ref[...] = own.astype(jnp.float32)
        heads_own = jnp.where(own, heads, zero)
        heads_other = jnp.where(own, zero, heads)
        for k in range(parts):
            term = matmul(heads_own, qo_own_ref[k, HD:, :])
            term = term + matmul(heads_other, qo_other_ref[k, HD:, :])
            out_ref[:, k * part : (k + 1) * part] = term.astype(out_ref.dtype)


def attend(blocks, core, positions, gains, qo_own, qo_other, keys, values, slab_start):
    rows = positions.shape[0]
    cache = keys.shape[0]
    parts, _, part = qo_own.shape
    width = parts * part

    def whole(array):
        return pl.BlockSpec(
            array.shape, lambda i: (0,) * array.ndim, pipeline_mode=pl.Buffered(1)
        )

    fixed = (core, positions, gains, qo_own, qo_other)
    tile = pl.BlockSpec((KEY_TILE, HD), lambda i: (i, 0))
    return pl.pallas_call(
        functools.partial(attend_kernel, slab_start, parts),
        grid=(cache // KEY_TILE,),
        in_specs=[whole(array) for array in fixed] + [tile] * 2 + [whole(b) for b in blocks],
        out_specs=[
            pl.BlockSpec((rows, width), lambda i: (0, 0)),
            pl.BlockSpec((rows, 1), lambda i: (0, 0)),
        ],
        out_shape=[
            jax.ShapeDtypeStruct((rows, width), jnp.bfloat16),
            jax.ShapeDtypeStruct((rows, 1), jnp.float32),
        ],
        scratch_shapes=[
            pltpu.VMEM((rows, blocks[0].shape[1]), jnp.bfloat16),
            pltpu.VMEM((rows, HD), jnp.bfloat16),
            pltpu.VMEM((rows, HD), jnp.float32),
            pltpu.VMEM((rows, HD), jnp.float32),
        ],
        compiler_params=pltpu.CompilerParams(vmem_limit_bytes=28 * 1024 * 1024),
        cost_estimate=pl.CostEstimate(
            flops=rows * width,
            bytes_accessed=rows * width,
            transcendentals=0,
        ),
        name="attend",
    )(*fixed, keys, values, *blocks)


def ffn_kernel(places, own_ref, *rest):
    n_pieces = 2 * len(places)
    pieces, rest = rest[:n_pieces], rest[n_pieces:]
    *blocks, out_ref, slab_ref, weights, gate_up, sems = rest
    units = weights.shape[2] // 3
    part = weights.shape[3]
    own = own_ref[...] > 0.5
    copies = []
    for index, (slot, low, high) in enumerate(places):
        for group in range(2):
            at = group * len(places) + index
            copy = pltpu.make_async_copy(
                pieces[at], weights.at[group, slot, :, low:high], sems.at[at]
            )
            copy.start()
            copies.append((slot, copy))
    fill(slab_ref, blocks)
    for slot in range(4):
        for place, copy in copies:
            if place == slot:
                copy.wait()
        rows = slab_ref[:, slot * part : (slot + 1) * part]
        for group in range(2):
            for kind in range(2):
                product = matmul_t(rows, weights[group, slot, kind * units : (kind + 1) * units, :])
                if slot == 0:
                    gate_up[group, kind] = product
                else:
                    gate_up[group, kind] += product
    gate = jnp.where(own, gate_up[0, 0], gate_up[1, 0])
    up = jnp.where(own, gate_up[0, 1], gate_up[1, 1])
    activated = (gate / (1.0 + jnp.exp(-gate)) * up).astype(jnp.bfloat16)
    zero = jnp.zeros_like(activated)
    activated_own = jnp.where(own, activated, zero)
    activated_other = jnp.where(own, zero, activated)
    for slot in range(4):
        term = matmul(activated_own, weights[0, slot, 2 * units :, :])
        term = term + matmul(activated_other, weights[1, slot, 2 * units :, :])
        out_ref[:, slot * part : (slot + 1) * part] = term.astype(out_ref.dtype)


def feed_forward(blocks, own, pieces_own, pieces_other, places):
    rows, width = own.shape[0], blocks[0].shape[1]
    stacked = pieces_own[0].shape[0]
    part = width // 4
    pieces = list(pieces_own) + list(pieces_other)
    return pl.pallas_call(
        functools.partial(ffn_kernel, places),
        in_specs=[pl.BlockSpec(memory_space=pltpu.VMEM)]
        + [pl.BlockSpec(memory_space=pl.ANY)] * len(pieces)
        + [pl.BlockSpec(memory_space=pltpu.VMEM)] * len(blocks),
        out_specs=pl.BlockSpec(memory_space=pltpu.VMEM),
        out_shape=jax.ShapeDtypeStruct((rows, width), jnp.bfloat16),
        scratch_shapes=[
            pltpu.VMEM((rows, width), jnp.bfloat16),
            pltpu.VMEM((2, 4, stacked, part), jnp.bfloat16),
            pltpu.VMEM((2, 2, rows, stacked // 3), jnp.float32),
            pltpu.SemaphoreType.DMA((len(pieces),)),
        ],
        compiler_params=pltpu.CompilerParams(vmem_limit_bytes=60 * 1024 * 1024),
        cost_estimate=pl.CostEstimate(
            flops=4 * rows * stacked * width,
            bytes_accessed=4 * stacked * width + 6 * rows * width,
            transcendentals=rows * stacked,
        ),
        name="feed_forward",
    )(own, *pieces, *blocks)


def per_device(
    hidden_in,
    query_modality,
    key_cache,
    value_cache,
    key_modality,
    norm_attn,
    query_weight,
    query_gain,
    key_gain,
    out_weight,
    norm_ffn,
    gate_weight,
    up_weight,
    down_weight,
):
    core = lax.axis_index("mod")
    ctx_index = lax.axis_index("ctx")
    n_ctx = lax.axis_size("ctx")
    n_x = lax.axis_size("dp")
    n_z = n_ctx // Y
    rows_dev, width = hidden_in.shape[1:]
    part = width // n_x
    cache_len = key_cache.shape[1]
    slab_len = rows_dev * n_ctx * lax.axis_size("mod")
    slab_start = cache_len - slab_len
    turn = lax.axis_index("dp") * part

    flags = jnp.broadcast_to(narrow(query_modality[0][:, None]), (rows_dev, HD))
    rows = gather_y(jnp.concatenate([hidden_in[0], flags], axis=1))

    qo_here = jnp.concatenate([query_weight[0].T, out_weight[0]], axis=0)
    qo_own = jnp.stack([qo_here] + [from_x(qo_here, k) for k in range(1, n_x)])
    qo_other = swap_core(qo_own)

    packed = jnp.concatenate([norm_attn, norm_ffn, query_gain], axis=1)
    packed_other = swap_core(packed)
    gains = jnp.concatenate(
        [norm_attn, packed_other[:, :width], norm_ffn, packed_other[:, width : 2 * width]], axis=0
    )
    gains = jnp.roll(gains, -turn, axis=1)
    q_gains = jnp.concatenate([query_gain, packed_other[:, 2 * width :]], axis=0)

    flags = rows[:, width:]
    rows_own = flags[:, :1] == narrow(core)
    hidden = wide(jnp.roll(rows[:, :width], -turn, axis=1))
    normed = narrow(rms_scale(hidden, jnp.where(rows_own, gains[0:1], gains[1:2])))
    block = jnp.concatenate([normed, flags], axis=1)

    padding = ((0, -down_weight.shape[1] % TILE), (0, 0))

    def stacked(low, high):
        weights = (gate_weight[0].T, up_weight[0].T, down_weight[0])
        return jnp.concatenate([jnp.pad(w[:, low:high], padding) for w in weights], axis=0)

    cut = part // 4
    here = [stacked(q * cut, (q + 1) * cut) for q in range(4)]
    own_pieces = {(0, None): stacked(0, part)}
    other_pieces = {(0, None): swap_core(own_pieces[0, None])}
    groups = [((1, q), (3, 3 - q)) for q in range(4)] + [((2, q), (2, 3 - q)) for q in range(2)]
    for index, group in enumerate(groups):
        sources = []
        for slot, q in group:
            if slot == 2:
                sources.append(own_pieces[(1 if q < 2 else 3), q])
            else:
                sources.append(here[q])
        waits = [rows]
        if index > 0:
            waits = [own_pieces[key] for key in groups[index - 1]]
        if index > 1:
            waits += [other_pieces[key] for key in groups[index - 2]]
        sources = after(sources, waits)
        for (slot, q), source in zip(group, sources):
            shift = slot if slot != 2 else (1 if q < 2 else 3)
            own_pieces[slot, q] = from_x(source, shift)
            other_pieces[slot, q] = swap_core(own_pieces[slot, q])

    def pull(moving):
        arrived = [own_pieces[key] for key in groups[-1]]
        moving, arrived = lax.optimization_barrier((moving, arrived))
        for key, piece in zip(groups[-1], arrived):
            own_pieces[key] = piece
        return moving

    blocks = gather_z(block, {})

    key_rows = after(key_cache[0], rows)
    key_scale = jnp.where(
        key_modality[0][:, None] == 0, key_gain[0][None, :], key_gain[1][None, :]
    )
    keys = narrow(rms_scale(wide(key_rows), key_scale))

    z_here, y_here = ctx_index // Y, ctx_index % Y
    at_z = (z_here + jnp.arange(n_z, dtype=jnp.int32)) % n_z
    at_y = (y_here + jnp.arange(Y, dtype=jnp.int32)) % Y
    at = core * n_ctx + at_z[:, None] * Y + at_y[None, :]
    positions = at[:, :, None] * rows_dev + jnp.arange(rows_dev, dtype=jnp.int32)
    positions = slab_start + positions.reshape(-1, 1)
    attended, slab_own = attend(
        blocks,
        wide(core).reshape(1, 1),
        positions,
        q_gains,
        qo_own,
        qo_other,
        keys,
        value_cache[0],
        slab_start,
    )
    attended = sum_y(scatter_z(attended, {}))

    residual = hidden + attended
    normed = narrow(rms_scale(residual, jnp.where(rows_own, gains[2:3], gains[3:4])))
    blocks = gather_z(normed, {3: pull})

    keys_of = sorted(own_pieces, key=lambda key: (key[0], key[1] or 0))
    places = tuple(
        (slot, 0, part) if q is None else (slot, q * cut, (q + 1) * cut) for slot, q in keys_of
    )
    mixed = feed_forward(
        blocks,
        slab_own,
        [own_pieces[key] for key in keys_of],
        [other_pieces[key] for key in keys_of],
        places,
    )
    mixed = scatter_y(scatter_z(mixed, {}))
    mixed = narrow(residual[:rows_dev] + mixed)
    return jnp.roll(mixed, turn, axis=1)[None]


def solution(mesh):
    placed = (
        P("dp", ("mod", "ctx"), None),
        P("dp", ("mod", "ctx")),
        P("dp", None, "ctx"),
        P("dp", None, "ctx"),
        P("dp", None),
        P("mod", None),
        P("mod", "dp", "ctx"),
        P("mod", "ctx"),
        P(None, "ctx"),
        P("mod", "ctx", "dp"),
        P("mod", None),
        P("mod", "dp", "ctx"),
        P("mod", "dp", "ctx"),
        P("mod", "ctx", "dp"),
    )
    return jax.shard_map(
        per_device,
        mesh=mesh,
        in_specs=placed,
        out_specs=P("dp", ("mod", "ctx"), None),
        check_vma=False,
    )
```

```python
import functools
import math

import jax
import jax.numpy as jnp
from jax import lax
from jax.experimental import pallas as pl
from jax.experimental.pallas import tpu as pltpu
from jax.sharding import PartitionSpec as P

HD = 128
Y = 4
KEY_TILE = 1024
TILE = 16

epsilon = 1e-05


def rms_scale(values, scales):
    inverse = lax.rsqrt(jnp.mean(values * values, axis=-1, keepdims=True) + epsilon)
    return values * inverse * scales


def swap_core(value):
    return lax.ppermute(value, "mod", [(0, 1), (1, 0)])


def from_x(value, shift):
    n_x = lax.axis_size("dp")
    return lax.ppermute(value, "dp", [((i + shift) % n_x, i) for i in range(n_x)])


def after(value, anchor):
    return lax.optimization_barrier((value, anchor))[0]


def from_yz(value, shift_y, shift_z):
    n_z = lax.axis_size("ctx") // Y
    pairs = [
        (((z + shift_z) % n_z) * Y + (y + shift_y) % Y, z * Y + y)
        for z in range(n_z)
        for y in range(Y)
    ]
    return lax.ppermute(value, "ctx", pairs)


def from_y(value, shift):
    return from_yz(value, shift, 0)


def from_z(value, shift):
    return from_yz(value, 0, shift)


def gather_y(block):
    return jnp.concatenate([block] + [from_y(block, dy) for dy in range(1, Y)], axis=0)


def gather_z(here, hooks):
    n_z = lax.axis_size("ctx") // Y
    top = n_z // 2
    half = here.shape[0] // 2
    blocks = {0: here}
    ahead = behind = here
    for step in range(1, top):
        ahead = from_z(ahead, 1)
        behind = from_z(behind, -1)
        if step in hooks:
            ahead = hooks[step](ahead)
        blocks[step] = ahead
        blocks[n_z - step] = behind
    far = [from_z(ahead[:half], 1), from_z(behind[half:], -1)]
    near = [blocks[dz] for dz in range(n_z) if dz != top]
    return near[:top] + far + near[top:]


def narrow(value):
    return value.astype(jnp.bfloat16)


def wide(value):
    return value.astype(jnp.float32)


def scatter_z(terms, hooks):
    n_z = lax.axis_size("ctx") // Y
    top = n_z // 2
    terms = terms.reshape(n_z, -1, terms.shape[-1])
    half = terms.shape[1] // 2
    ahead = from_z(terms[top][:half], -1)
    behind = from_z(terms[top][half:], 1)
    for step in range(top - 1, 0, -1):
        own_ahead, own_behind = terms[step], terms[n_z - step]
        if step == top - 1:
            first = narrow(wide(ahead) + wide(own_ahead[:half]))
            ahead = jnp.concatenate([first, own_ahead[half:]], axis=0)
            first = narrow(wide(behind) + wide(own_behind[half:]))
            behind = jnp.concatenate([own_behind[:half], first], axis=0)
        else:
            ahead = narrow(wide(ahead) + wide(own_ahead))
            behind = narrow(wide(behind) + wide(own_behind))
        ahead = from_z(ahead, -1)
        behind = from_z(behind, 1)
        if step in hooks:
            ahead = hooks[step](ahead)
    return wide(terms[0]) + wide(ahead) + wide(behind)


def scatter_y(total):
    total = total.reshape(Y, -1, total.shape[-1])
    result = total[0]
    for dy in range(1, Y):
        result = result + wide(from_y(narrow(total[dy]), -dy))
    return result


def sum_y(total):
    sent = narrow(total)
    rows = total.shape[0] // Y
    result = total
    for dy in range(1, Y):
        result = result + jnp.roll(wide(from_y(sent, dy)), dy * rows, axis=0)
    return result


def matmul(left, right):
    return jnp.dot(left, right, preferred_element_type=jnp.float32)


def matmul_t(left, right):
    return lax.dot_general(
        left, right, (((1,), (1,)), ((), ())), preferred_element_type=jnp.float32
    )


def fill(slab, blocks):
    low = 0
    for block in blocks:
        slab[low : low + block.shape[0], :] = block[...]
        low += block.shape[0]


def attend_kernel(
    slab_start,
    parts,
    core_ref,
    position_ref,
    gain_ref,
    qo_own_ref,
    qo_other_ref,
    key_ref,
    value_ref,
    *rest,
):
    *blocks, out_ref, own_ref, slab_ref, query, summed, row_total = rest
    step = pl.program_id(0)
    last = pl.num_programs(0) - 1
    part = qo_own_ref.shape[2]
    width = parts * part
    sub = KEY_TILE // 2

    def is_own():
        return slab_ref[:, width : width + 1].astype(jnp.float32) == core_ref[...]

    @pl.when(step == 0)
    def _():
        fill(slab_ref, blocks)
        own = is_own()
        projected_own = projected_other = 0.0
        for k in range(parts):
            rows = slab_ref[:, k * part : (k + 1) * part]
            projected_own = projected_own + matmul_t(rows, qo_own_ref[k, :HD, :])
            projected_other = projected_other + matmul_t(rows, qo_other_ref[k, :HD, :])
        projected = jnp.where(own, projected_own, projected_other)
        gain = jnp.where(own, gain_ref[0:1, :], gain_ref[1:2, :])
        normed = rms_scale(projected, gain)
        query[...] = (normed * (math.log2(math.e) / math.sqrt(HD))).astype(jnp.bfloat16)
        summed[...] = jnp.zeros_like(summed)
        row_total[...] = jnp.zeros_like(row_total)

    def add_keys(masked):
        for index in range(KEY_TILE // sub):
            scores = matmul_t(query[...], key_ref[index * sub : (index + 1) * sub, :])
            weights = jnp.exp2(scores)
            if masked:
                at = step * KEY_TILE + index * sub
                ids = at + lax.broadcasted_iota(jnp.int32, scores.shape, 1)
                weights = jnp.where(ids <= position_ref[...], weights, 0.0)
            folded = weights[:, :HD]
            for lane in range(HD, sub, HD):
                folded = folded + weights[:, lane : lane + HD]
            row_total[...] += folded
            summed[...] += matmul(
                weights.astype(jnp.bfloat16), value_ref[index * sub : (index + 1) * sub, :]
            )

    first_masked = slab_start // KEY_TILE

    @pl.when(step < first_masked)
    def _():
        add_keys(False)

    @pl.when(step >= first_masked)
    def _():
        add_keys(True)

    @pl.when(step == last)
    def _():
        totals = jnp.sum(row_total[...], axis=-1, keepdims=True)
        heads = (summed[...] / totals).astype(jnp.bfloat16)
        zero = jnp.zeros_like(heads)
        own = is_own()
        own_ref[...] = own.astype(jnp.float32)
        heads_own = jnp.where(own, heads, zero)
        heads_other = jnp.where(own, zero, heads)
        for k in range(parts):
            term = matmul(heads_own, qo_own_ref[k, HD:, :])
            term = term + matmul(heads_other, qo_other_ref[k, HD:, :])
            out_ref[:, k * part : (k + 1) * part] = term.astype(out_ref.dtype)


def attend(blocks, core, positions, gains, qo_own, qo_other, keys, values, slab_start):
    rows = positions.shape[0]
    cache = keys.shape[0]
    parts, _, part = qo_own.shape
    width = parts * part

    def whole(array):
        return pl.BlockSpec(
            array.shape, lambda i: (0,) * array.ndim, pipeline_mode=pl.Buffered(1)
        )

    fixed = (core, positions, gains, qo_own, qo_other)
    tile = pl.BlockSpec((KEY_TILE, HD), lambda i: (i, 0))
    return pl.pallas_call(
        functools.partial(attend_kernel, slab_start, parts),
        grid=(cache // KEY_TILE,),
        in_specs=[whole(array) for array in fixed] + [tile] * 2 + [whole(b) for b in blocks],
        out_specs=[
            pl.BlockSpec((rows, width), lambda i: (0, 0)),
            pl.BlockSpec((rows, 1), lambda i: (0, 0)),
        ],
        out_shape=[
            jax.ShapeDtypeStruct((rows, width), jnp.bfloat16),
            jax.ShapeDtypeStruct((rows, 1), jnp.float32),
        ],
        scratch_shapes=[
            pltpu.VMEM((rows, blocks[0].shape[1]), jnp.bfloat16),
            pltpu.VMEM((rows, HD), jnp.bfloat16),
            pltpu.VMEM((rows, HD), jnp.float32),
            pltpu.VMEM((rows, HD), jnp.float32),
        ],
        compiler_params=pltpu.CompilerParams(vmem_limit_bytes=28 * 1024 * 1024),
        cost_estimate=pl.CostEstimate(
            flops=rows * width,
            bytes_accessed=rows * width,
            transcendentals=0,
        ),
        name="attend",
    )(*fixed, keys, values, *blocks)


def ffn_kernel(places, own_ref, *rest):
    n_pieces = 2 * len(places)
    pieces, rest = rest[:n_pieces], rest[n_pieces:]
    *blocks, out_ref, slab_ref, weights, gate_up, sems = rest
    units = weights.shape[2] // 3
    part = weights.shape[3]
    own = own_ref[...] > 0.5
    copies = []
    for index, (slot, low, high) in enumerate(places):
        for group in range(2):
            at = group * len(places) + index
            copy = pltpu.make_async_copy(
                pieces[at], weights.at[group, slot, :, low:high], sems.at[at]
            )
            copy.start()
            copies.append((slot, copy))
    fill(slab_ref, blocks)
    for slot in range(4):
        for place, copy in copies:
            if place == slot:
                copy.wait()
        rows = slab_ref[:, slot * part : (slot + 1) * part]
        for group in range(2):
            product = matmul_t(rows, weights[group, slot, : 2 * units, :])
            if slot == 0:
                gate_up[group] = product
            else:
                gate_up[group] += product
    both = jnp.where(own, gate_up[0], gate_up[1])
    gate, up = both[:, :units], both[:, units:]
    activated = (gate / (1.0 + jnp.exp(-gate)) * up).astype(jnp.bfloat16)
    zero = jnp.zeros_like(activated)
    activated_own = jnp.where(own, activated, zero)
    activated_other = jnp.where(own, zero, activated)
    for slot in range(4):
        term = matmul(activated_own, weights[0, slot, 2 * units :, :])
        term = term + matmul(activated_other, weights[1, slot, 2 * units :, :])
        out_ref[:, slot * part : (slot + 1) * part] = term.astype(out_ref.dtype)


def feed_forward(blocks, own, pieces_own, pieces_other, places):
    rows, width = own.shape[0], blocks[0].shape[1]
    stacked = pieces_own[0].shape[0]
    part = width // 4
    pieces = list(pieces_own) + list(pieces_other)
    return pl.pallas_call(
        functools.partial(ffn_kernel, places),
        in_specs=[pl.BlockSpec(memory_space=pltpu.VMEM)]
        + [pl.BlockSpec(memory_space=pl.ANY)] * len(pieces)
        + [pl.BlockSpec(memory_space=pltpu.VMEM)] * len(blocks),
        out_specs=pl.BlockSpec(memory_space=pltpu.VMEM),
        out_shape=jax.ShapeDtypeStruct((rows, width), jnp.bfloat16),
        scratch_shapes=[
            pltpu.VMEM((rows, width), jnp.bfloat16),
            pltpu.VMEM((2, 4, stacked, part), jnp.bfloat16),
            pltpu.VMEM((2, rows, 2 * stacked // 3), jnp.float32),
            pltpu.SemaphoreType.DMA((len(pieces),)),
        ],
        compiler_params=pltpu.CompilerParams(vmem_limit_bytes=60 * 1024 * 1024),
        cost_estimate=pl.CostEstimate(
            flops=4 * rows * stacked * width,
            bytes_accessed=4 * stacked * width + 6 * rows * width,
            transcendentals=rows * stacked,
        ),
        name="feed_forward",
    )(own, *pieces, *blocks)


def per_device(
    hidden_in,
    query_modality,
    key_cache,
    value_cache,
    key_modality,
    norm_attn,
    query_weight,
    query_gain,
    key_gain,
    out_weight,
    norm_ffn,
    gate_weight,
    up_weight,
    down_weight,
):
    core = lax.axis_index("mod")
    ctx_index = lax.axis_index("ctx")
    n_ctx = lax.axis_size("ctx")
    n_x = lax.axis_size("dp")
    n_z = n_ctx // Y
    rows_dev, width = hidden_in.shape[1:]
    part = width // n_x
    cache_len = key_cache.shape[1]
    slab_len = rows_dev * n_ctx * lax.axis_size("mod")
    slab_start = cache_len - slab_len
    turn = lax.axis_index("dp") * part

    flags = jnp.broadcast_to(narrow(query_modality[0][:, None]), (rows_dev, HD))
    rows = gather_y(jnp.concatenate([hidden_in[0], flags], axis=1))

    qo_here = jnp.concatenate([query_weight[0].T, out_weight[0]], axis=0)
    qo_own = jnp.stack([qo_here] + [from_x(qo_here, k) for k in range(1, n_x)])
    qo_other = swap_core(qo_own)

    packed = jnp.concatenate([norm_attn, norm_ffn, query_gain], axis=1)
    packed_other = swap_core(packed)
    gains = jnp.concatenate(
        [norm_attn, packed_other[:, :width], norm_ffn, packed_other[:, width : 2 * width]], axis=0
    )
    gains = jnp.roll(gains, -turn, axis=1)
    q_gains = jnp.concatenate([query_gain, packed_other[:, 2 * width :]], axis=0)

    flags = rows[:, width:]
    rows_own = flags[:, :1] == narrow(core)
    hidden = wide(jnp.roll(rows[:, :width], -turn, axis=1))
    normed = narrow(rms_scale(hidden, jnp.where(rows_own, gains[0:1], gains[1:2])))
    block = jnp.concatenate([normed, flags], axis=1)

    padding = ((0, -down_weight.shape[1] % TILE), (0, 0))

    gate_weight, up_weight, down_weight = after((gate_weight, up_weight, down_weight), rows)

    def stacked(low, high):
        weights = (gate_weight[0].T, up_weight[0].T, down_weight[0])
        return jnp.concatenate([jnp.pad(w[:, low:high], padding) for w in weights], axis=0)

    cut = part // 4
    here = [stacked(q * cut, (q + 1) * cut) for q in range(4)]
    own_pieces = {(0, None): stacked(0, part)}
    other_pieces = {(0, None): swap_core(own_pieces[0, None])}
    groups = [((1, q), (3, 3 - q)) for q in range(4)] + [((2, q), (2, 3 - q)) for q in range(2)]
    for index, group in enumerate(groups):
        sources = []
        for slot, q in group:
            if slot == 2:
                sources.append(own_pieces[(1 if q < 2 else 3), q])
            else:
                sources.append(here[q])
        waits = [rows]
        if 0 < index < len(groups) - 1:
            waits = [own_pieces[key] for key in groups[index - 1]]
        if index > 1:
            waits += [other_pieces[key] for key in groups[index - 2]]
        sources = after(sources, waits)
        for (slot, q), source in zip(group, sources):
            shift = slot if slot != 2 else (1 if q < 2 else 3)
            own_pieces[slot, q] = from_x(source, shift)
            other_pieces[slot, q] = swap_core(own_pieces[slot, q])

    def pull(index):
        def hook(moving):
            arrived = [own_pieces[key] for key in groups[index]]
            moving, arrived = lax.optimization_barrier((moving, arrived))
            own_pieces.update(zip(groups[index], arrived))
            return moving

        return hook

    blocks = pull(0)(gather_z(block, {}))

    key_rows = after(key_cache[0], rows)
    key_scale = jnp.where(
        key_modality[0][:, None] == 0, key_gain[0][None, :], key_gain[1][None, :]
    )
    keys = narrow(rms_scale(wide(key_rows), key_scale))

    z_here, y_here = ctx_index // Y, ctx_index % Y
    at_z = (z_here + jnp.arange(n_z, dtype=jnp.int32)) % n_z
    at_y = (y_here + jnp.arange(Y, dtype=jnp.int32)) % Y
    at = core * n_ctx + at_z[:, None] * Y + at_y[None, :]
    positions = at[:, :, None] * rows_dev + jnp.arange(rows_dev, dtype=jnp.int32)
    positions = slab_start + positions.reshape(-1, 1)
    attended, slab_own = attend(
        blocks,
        wide(core).reshape(1, 1),
        positions,
        q_gains,
        qo_own,
        qo_other,
        keys,
        value_cache[0],
        slab_start,
    )
    attended = sum_y(scatter_z(attended, {}))

    residual = hidden + attended
    normed = narrow(rms_scale(residual, jnp.where(rows_own, gains[2:3], gains[3:4])))
    blocks = gather_z(normed, {1: pull(-2), 3: pull(-1)})

    keys_of = sorted(own_pieces, key=lambda key: (key[0], key[1] or 0))
    places = tuple(
        (slot, 0, part) if q is None else (slot, q * cut, (q + 1) * cut) for slot, q in keys_of
    )
    mixed = feed_forward(
        blocks,
        slab_own,
        [own_pieces[key] for key in keys_of],
        [other_pieces[key] for key in keys_of],
        places,
    )
    mixed = scatter_y(scatter_z(mixed, {}))
    mixed = narrow(residual[:rows_dev] + mixed)
    return jnp.roll(mixed, turn, axis=1)[None]


def solution(mesh):
    placed = (
        P("dp", ("mod", "ctx"), None),
        P("dp", ("mod", "ctx")),
        P("dp", None, "ctx"),
        P("dp", None, "ctx"),
        P("dp", None),
        P("mod", None),
        P("mod", "dp", "ctx"),
        P("mod", "ctx"),
        P(None, "ctx"),
        P("mod", "ctx", "dp"),
        P("mod", None),
        P("mod", "dp", "ctx"),
        P("mod", "dp", "ctx"),
        P("mod", "ctx", "dp"),
    )
    return jax.shard_map(
        per_device,
        mesh=mesh,
        in_specs=placed,
        out_specs=P("dp", ("mod", "ctx"), None),
        check_vma=False,
    )
```
